32 devices in a mesh: dp: 4 (over z), pipe: 4 (over y, x), tensor: 2 (over core).
Axes of the slice: x: 2, y: 2, z: 4, core: 2. Of those that a mesh axis runs over, the one named last changes fastest.
Arguments:
- section_out: bfloat16 [4, 512, 12288], P('pipe', 'dp', 'tensor'), may hold values from -6 to 6
- embedded: bfloat16 [512, 12288], P('dp', 'tensor'), may hold values from -6 to 6
- cot_norm: bfloat16 [4, 512, 12288], P('pipe', 'dp', 'tensor'), may hold values from -3 to 3
- cot_res: bfloat16 [4, 512, 12288], P('pipe', 'dp', 'tensor'), may hold values from -3 to 3
- gain: bfloat16 [4, 64, 12288], P('pipe', None, 'tensor'), may hold values from 0.25 to 1.75
- bias: bfloat16 [4, 64, 12288], P('pipe', None, 'tensor'), may hold values from -1.5 to 1.5
- lang_ids: int32 [512], P('dp'), may hold values from 0 to 63
- mb_order: int32 [4, 4], P('dp'), may hold values from 0 to 3, each once within a row
Outputs:
- normed_out: bfloat16 [4, 512, 12288], P('pipe', 'dp', 'tensor')
- returned_grad: bfloat16 [4, 512, 12288], P('pipe', 'dp', 'tensor')
- gain_grad: float32 [4, 64, 12288], P('pipe', None, 'tensor')
- bias_grad: float32 [4, 64, 12288], P('pipe', None, 'tensor')
The draws below stay inside these ranges and needn't reach their ends.
Inputs may be any that keep to these rules, and one draw needn't show every extreme that they name: `lang_ids`: a language id for every token. `mb_order`: each replica's row is a permutation of the 4 micro-batches.
All inputs are finite; a program needn't handle non-finite values.
Results may differ from the reference program's by a relative error of at most 0.0004.
Values may be sent and summed in bfloat16 or wider, within the bound.
A program may use at most 64 MiB of HBM per device.

```python
import math
import jax
import jax.numpy as jnp
import numpy as np
from jax import lax

D = 12288
LANGS = 64
MB = 4
ROWS = 32
TOKENS = 512
N_DP = 4
N_PIPE = 4


def touch_ends(entries, own_key, low, largest):
    shape = entries.shape
    index_at = [jax.random.randint(jax.random.fold_in(own_key, axis), (), 0, shape[axis]) for axis in range(len(shape))]
    entries = entries.at[tuple(index_at)].set(low)
    longest = shape.index(max(shape))
    index_at[longest] = (index_at[longest] + 1) % shape[longest]
    return entries.at[tuple(index_at)].set(largest)


def block_levels(own_key, dims, cuts, smallest, top_value):
    def one(position, shards_of):
        steps = jax.random.uniform(jax.random.fold_in(jax.random.fold_in(own_key, 6), position), (shards_of,), jnp.float32, smallest / len(cuts), top_value / len(cuts))
        return jnp.repeat(jnp.exp(steps), dims[position] // shards_of).reshape((-1,) + (1,) * (len(dims) - position - 1))

    level = one(*cuts[0])
    for cut in cuts[1:]:
        level = level * one(*cut)
    return level


def cumulative_ranks(count, slope):
    weights = [(1 << 20) // math.isqrt(standing ** slope) + 1 for standing in range(1, count + 1)]
    scale = 1 + sum(weights) // (1 << 30)
    return np.cumsum(np.array([max(1, weight // scale) for weight in weights]))


def skewed_ids(own_key, extent, amount, lean):
    listing = cumulative_ranks(amount, lean)
    ticket = jax.random.randint(jax.random.fold_in(own_key, 1), extent, 0, int(listing[amount - 1]))
    rank = jnp.searchsorted(jnp.asarray(listing, jnp.int32), ticket, side="right")
    return jax.random.permutation(jax.random.fold_in(own_key, 2), amount)[rank].astype(jnp.int32)


def bell_draw(rng, shape, deviation, reach, split=(), kind=jnp.bfloat16):
    level = block_levels(rng, shape, split, -0.22, 0.18) if split else 1.0
    entries = jax.random.normal(rng, shape, jnp.float32) * deviation * level
    return jnp.minimum(jnp.maximum(entries, -reach), reach).astype(kind)


def setup_inputs(seed: int = 0) -> dict:
    streams_of = jax.random.split(jax.random.key(seed), 9)
    section_out = bell_draw(streams_of[0], (N_PIPE, TOKENS, D), 1.0, 6.0, ((0, 4), (1, 4), (2, 2)))
    embedded = bell_draw(streams_of[1], (TOKENS, D), 1.0, 6.0, ((0, 4), (1, 2)))
    cot_norm = bell_draw(streams_of[2], (N_PIPE, TOKENS, D), 0.5, 3.0, ((0, 4), (1, 4), (2, 2)))
    cot_res = bell_draw(streams_of[3], (N_PIPE, TOKENS, D), 0.5, 3.0, ((0, 4), (1, 4), (2, 2)))
    gain = jnp.clip(1.0 + 0.15 * jax.random.normal(streams_of[4], (N_PIPE, LANGS, D), jnp.float32), 0.25, 1.75).astype(jnp.bfloat16)
    bias = bell_draw(streams_of[5], (N_PIPE, LANGS, D), 0.3, 1.5, ((0, 4), (2, 2)))
    lang_ids = touch_ends(skewed_ids(streams_of[6], (TOKENS,), LANGS, 1), jax.random.fold_in(streams_of[6], 3), 0, LANGS - 1).astype(jnp.int32)
    mb_order = jax.vmap(lambda own: jax.random.permutation(own, MB))(jax.random.split(streams_of[7], N_DP)).reshape((N_DP, MB)).astype(jnp.int32)
    return {"section_out": section_out, "embedded": embedded, "cot_norm": cot_norm, "cot_res": cot_res, "gain": gain, "bias": bias, "lang_ids": lang_ids, "mb_order": mb_order}


eps = 1e-05

def blocks_take(values, order):
    shaped = values.reshape((N_DP, MB, ROWS) + values.shape[1:])
    replica = jnp.arange(N_DP, dtype=jnp.int32)[:, None]
    return shaped[replica, order].reshape(values.shape)

def inverse_of(order):
    slots = jnp.arange(MB, dtype=jnp.int32)
    hits = (order[:, :, None] == slots[None, None, :]).astype(jnp.int32)
    return lax.optimization_barrier(jnp.sum(slots[None, :, None] * hits, axis=1)).astype(jnp.int32)

def one_section(section_in, cot_norm, cot_res, gain, bias, lang_ids, mb_order):
    inputs = section_in.astype(jnp.float32)
    moment_one = lax.optimization_barrier(jnp.sum(inputs, axis=1, keepdims=True))
    moment_two = lax.optimization_barrier(jnp.sum(inputs * inputs, axis=1, keepdims=True))
    center = moment_one / D
    spread = moment_two / D - center * center
    inv_scale = lax.rsqrt(spread + eps)
    normalized = (inputs - center) * inv_scale
    gain_rows = gain[lang_ids].astype(jnp.float32)
    bias_rows = bias[lang_ids].astype(jnp.float32)
    normed = (normalized * gain_rows + bias_rows).astype(jnp.bfloat16)
    inverse = inverse_of(mb_order)
    cot_fwd = blocks_take(cot_norm, inverse).astype(jnp.float32)
    pass_fwd = blocks_take(cot_res, inverse).astype(jnp.float32)
    scaled_cot = cot_fwd * gain_rows
    mean_cot = lax.optimization_barrier(jnp.sum(scaled_cot, axis=1, keepdims=True)) / D
    mean_cross = lax.optimization_barrier(jnp.sum(scaled_cot * normalized, axis=1, keepdims=True)) / D
    input_grad = (pass_fwd + inv_scale * (scaled_cot - mean_cot - normalized * mean_cross)).astype(jnp.bfloat16)
    input_grad = blocks_take(input_grad, mb_order)
    gain_part = jax.ops.segment_sum(cot_fwd * normalized, lang_ids, num_segments=LANGS)
    bias_part = jax.ops.segment_sum(cot_fwd, lang_ids, num_segments=LANGS)
    return (normed, input_grad, gain_part, bias_part)

def reference(section_out, embedded, cot_norm, cot_res, gain, bias, lang_ids, mb_order):
    section_in = jnp.concatenate([embedded[None], section_out[:-1]], axis=0)

    def apply(items):
        return one_section(items[0], items[1], items[2], items[3], items[4], lang_ids, mb_order)
    normed, input_grad, gain_grad, bias_grad = lax.map(apply, (section_in, cot_norm, cot_res, gain, bias))
    returned_grad = jnp.roll(input_grad, -1, axis=0)
    return (normed, returned_grad, gain_grad, bias_grad)
```

```python
import functools

import jax
import jax.numpy as jnp
from jax import lax
from jax.experimental import pallas as pl
from jax.experimental.pallas import tpu as pltpu
from jax.sharding import PartitionSpec as P

D = 12288
MB = 4
EPS = 1e-05
CW = 384
AHEAD = 4
LANES = 128
MESH = pl.DeviceIdType.MESH
ANY = pl.BlockSpec(memory_space=pl.ANY)
VMEM = pl.BlockSpec(memory_space=pltpu.VMEM)
SMEM = pl.BlockSpec(memory_space=pltpu.SMEM)
F32 = jnp.float32
BF16 = jnp.bfloat16


def fold(value):
    total = value[:, :LANES]
    for start in range(LANES, value.shape[1], LANES):
        total = total + value[:, start : start + LANES]
    return total


def pack(first, second):
    lane = lax.broadcasted_iota(jnp.int32, first.shape, 1)
    one = jnp.sum(first, axis=1, keepdims=True)
    two = jnp.sum(second, axis=1, keepdims=True)
    return jnp.where(lane == 0, one, jnp.where(lane == 1, two, 0.0))


def kernel(
    n_dp, n_pipe, n_tensor,
    section, embedded, cot, res, gain, bias, lang, order,
    normed_out, grad_out, gain_out, bias_out,
    source, cot_raw, res_raw, x_buf, cot_fwd, xn_buf, sc_buf, n_buf, g_buf, g_tmp,
    own, came, tot, mom_own, mom_in, cross_own, cross_in, rows, sel_t2, sel,
    load_sem, x_send, x_recv, mom_send, mom_recv, cross_send, cross_recv,
    up_send, in_recv, tot_send, tot_recv, sum_out, n_out, g_send, g_recv,
):
    dp, pipe, tensor = lax.axis_index("dp"), lax.axis_index("pipe"), lax.axis_index("tensor")
    tokens, width = section.shape[1], section.shape[2]
    langs = gain.shape[0]
    per = tokens // MB
    count = width // CW
    half = n_dp // 2
    left = dp < half
    up = jnp.where(left, dp + 1, dp - 1)
    out = jnp.where(left, dp - 1, dp + 1)
    center = jnp.logical_or(dp == half - 1, dp == half)
    edge = jnp.logical_not(center)
    relay = jnp.logical_and(dp > 0, dp < n_dp - 1)
    after, before = lax.rem(pipe + 1, n_pipe), lax.rem(pipe + n_pipe - 1, n_pipe)
    first, last = pipe == 0, pipe == n_pipe - 1

    def columns(c):
        return pl.ds(pl.multiple_of(c * CW, CW), CW)

    @pl.when(last)
    def _():
        pltpu.make_async_copy(embedded, source, load_sem.at[0]).start()

    @pl.when(jnp.logical_not(last))
    def _():
        pltpu.make_async_copy(section.at[0], source, load_sem.at[0]).start()

    load_cot = pltpu.make_async_copy(cot, cot_raw, load_sem.at[1])
    load_res = pltpu.make_async_copy(res, res_raw, load_sem.at[2])
    load_cot.start()
    load_res.start()

    barrier = pltpu.get_barrier_semaphore()
    partners = 0
    for step in (1, n_dp - 1):
        pl.semaphore_signal(barrier, inc=1, device_id={"dp": lax.rem(dp + step, n_dp)}, device_id_type=MESH)
        partners += 1
    for t in range(n_tensor):
        other = lax.rem(tensor + t, n_tensor)
        for p in (after, before):
            pl.semaphore_signal(barrier, inc=1, device_id={"pipe": p, "tensor": other}, device_id_type=MESH)
            partners += 1
        if t:
            pl.semaphore_signal(barrier, inc=1, device_id={"tensor": other}, device_id_type=MESH)
            partners += 1

    picks = (lax.broadcasted_iota(jnp.int32, (langs, tokens), 0) == lang[...]).astype(F32)
    sel_t2[:, :tokens] = picks.astype(BF16)
    sel_t2[:, tokens:] = picks.astype(BF16)
    sel[...] = picks.T.astype(BF16)

    pltpu.make_async_copy(embedded, source, load_sem.at[0]).wait()
    zeros = jnp.zeros((tokens, LANES), F32)

    def moments(c, carry):
        x = source[:, columns(c)].astype(F32)
        return carry[0] + fold(x), carry[1] + fold(x * x)

    one, two = lax.fori_loop(0, count, moments, (zeros, zeros))
    mom_own[...] = pack(one, two)

    pl.semaphore_wait(barrier, partners)

    def send_moments(t):
        return pltpu.make_async_remote_copy(
            src_ref=mom_own, dst_ref=mom_in.at[tensor],
            send_sem=mom_send.at[t], recv_sem=mom_recv.at[tensor],
            device_id={"pipe": after, "tensor": lax.rem(tensor + t, n_tensor)}, device_id_type=MESH,
        )

    for t in range(n_tensor):
        send_moments(t).start()

    def send_x(c):
        return pltpu.make_async_remote_copy(
            src_ref=section.at[0, :, columns(c)], dst_ref=x_buf.at[c],
            send_sem=x_send.at[c], recv_sem=x_recv.at[c],
            device_id={"pipe": after}, device_id_type=MESH,
        )

    def load_x(c):
        return pltpu.make_async_copy(embedded.at[:, columns(c)], x_buf.at[c], x_recv.at[c])

    @pl.when(jnp.logical_not(last))
    def _():
        for c in range(min(AHEAD, count)):
            send_x(c).start()

    @pl.when(first)
    def _():
        @pl.loop(0, count)
        def _(c):
            load_x(c).start()

    def send_up(s):
        return pltpu.make_async_remote_copy(
            src_ref=own.at[s], dst_ref=came.at[s], send_sem=up_send.at[s], recv_sem=in_recv.at[s],
            device_id={"dp": up}, device_id_type=MESH,
        )

    def swap(s):
        return pltpu.make_async_remote_copy(
            src_ref=own.at[s], dst_ref=tot.at[s], send_sem=up_send.at[s], recv_sem=tot_recv.at[s],
            device_id={"dp": up}, device_id_type=MESH,
        )

    def send_total(s):
        return pltpu.make_async_remote_copy(
            src_ref=tot.at[s], dst_ref=tot.at[s], send_sem=tot_send.at[s], recv_sem=tot_recv.at[s],
            device_id={"dp": out}, device_id_type=MESH,
        )

    def partial_on(s):
        @pl.when(relay)
        def _():
            send_up(s).wait_recv()
            own[s] = own[s] + came[s]

        @pl.when(center)
        def _():
            swap(s).start()

        @pl.when(edge)
        def _():
            send_up(s).start()

    def total_on(s, target, c):
        swap(s).wait_recv()

        @pl.when(center)
        def _():
            tot[s] = tot[s] + own[s]

        @pl.when(relay)
        def _():
            send_total(s).start()

        pltpu.make_async_copy(tot.at[s], target.at[:, columns(c)], sum_out.at[s]).start()

    def totals(s):
        @pl.when(s < count)
        def _():
            total_on(s, bias_out, s)

        @pl.when(s >= count)
        def _():
            total_on(s, gain_out, s - count)

    lag = jnp.where(center, 2, 8)

    def slot(s):
        partial_on(s)

        @pl.when(s >= lag)
        def _():
            totals(s - lag)

    slots = [order[0, j] for j in range(MB)]
    place = []
    for m in range(MB):
        found = 0
        for j in range(MB):
            found = jnp.where(slots[j] == m, j, found)
        place.append(found)

    load_cot.wait()

    def bias_part(c):
        cols = columns(c)
        for m in range(MB):
            cot_fwd[c, m * per : (m + 1) * per, :] = cot_raw[place[m], :, cols]
        own[c] = jnp.dot(sel_t2[:, :tokens], cot_fwd[c], preferred_element_type=F32)

    for t in range(n_tensor):
        pltpu.make_async_remote_copy(
            src_ref=mom_own, dst_ref=mom_in.at[t], send_sem=mom_send.at[t], recv_sem=mom_recv.at[t],
            device_id={"pipe": after}, device_id_type=MESH,
        ).wait_recv()
    moment = mom_in[0]
    for t in range(1, n_tensor):
        moment = moment + mom_in[t]
    mean = moment[:, 0:1] / D
    spread = moment[:, 1:2] / D - mean * mean
    rows[0] = jnp.broadcast_to(mean, (tokens, LANES))
    rows[1] = jnp.broadcast_to(lax.rsqrt(spread + EPS), (tokens, LANES))
    cross_in[tensor] = zeros
    rows[2] = zeros
    rows[3] = zeros

    def wide(value):
        return jnp.concatenate([value] * (CW // LANES), axis=1)

    @pl.loop(0, count)
    def _(c):
        cols = columns(c)

        bias_part(c)
        slot(c)

        @pl.when(first)
        def _():
            load_x(c).wait()

        @pl.when(jnp.logical_not(first))
        def _():
            send_x(c).wait_recv()

        @pl.when(jnp.logical_not(last))
        def _():
            send_x(c).wait_send()

            @pl.when(c + AHEAD < count)
            def _():
                send_x(c + AHEAD).start()

        gain_rows = jnp.dot(sel[...], gain[:, cols], preferred_element_type=F32)
        bias_rows = jnp.dot(sel[...], bias[:, cols], preferred_element_type=F32)
        xn = (x_buf[c].astype(F32) - wide(rows[0])) * wide(rows[1])
        n_buf[c] = (xn * gain_rows + bias_rows).astype(BF16)
        pltpu.make_async_copy(n_buf.at[c], normed_out.at[:, cols], n_out.at[c]).start()
        ct = cot_fwd[c].astype(F32)
        sc = ct * gain_rows
        rows[2] = rows[2] + fold(sc)
        rows[3] = rows[3] + fold(sc * xn)
        xn_buf[c] = xn
        sc_buf[c] = sc
        product = ct * xn
        high = product.astype(BF16)
        low = (product - high.astype(F32)).astype(BF16)
        own[count + c] = jnp.dot(
            sel_t2[...], jnp.concatenate([high, low], axis=0), preferred_element_type=F32
        )

    cross_own[...] = pack(rows[2], rows[3])

    def send_cross(t):
        return pltpu.make_async_remote_copy(
            src_ref=cross_own, dst_ref=cross_in.at[tensor],
            send_sem=cross_send.at[t], recv_sem=cross_recv.at[tensor],
            device_id={"tensor": lax.rem(tensor + t, n_tensor)}, device_id_type=MESH,
        )

    for t in range(1, n_tensor):
        send_cross(t).start()
    slot(count)
    for t in range(1, n_tensor):
        other = lax.rem(tensor + t, n_tensor)
        pltpu.make_async_remote_copy(
            src_ref=cross_own, dst_ref=cross_in.at[other],
            send_sem=cross_send.at[t], recv_sem=cross_recv.at[other],
            device_id={"tensor": other}, device_id_type=MESH,
        ).wait_recv()
    cross = cross_own[...]
    for t in range(n_tensor):
        cross = cross + cross_in[t]
    rows[2] = jnp.broadcast_to(cross[:, 0:1] / D, (tokens, LANES))
    rows[3] = jnp.broadcast_to(cross[:, 1:2] / D, (tokens, LANES))
    load_res.wait()

    def send_grad(c):
        return pltpu.make_async_remote_copy(
            src_ref=g_buf.at[c], dst_ref=grad_out.at[:, columns(c)],
            send_sem=g_send.at[c], recv_sem=g_recv.at[c],
            device_id={"pipe": before}, device_id_type=MESH,
        )

    def grad_part(c):
        cols = columns(c)
        for m in range(MB):
            span = slice(m * per, (m + 1) * per)
            inner = sc_buf[c, span, :] - wide(rows[2, span, :]) - xn_buf[c, span, :] * wide(rows[3, span, :])
            g_tmp[m] = (
                res_raw[place[m], :, cols].astype(F32) + wide(rows[1, span, :]) * inner
            ).astype(BF16)
        for j in range(MB):
            g_buf[c, j * per : (j + 1) * per, :] = g_tmp[slots[j]]
        send_grad(c).start()

    both = count // 2

    @pl.loop(0, both)
    def _(i):
        grad_part(2 * i)
        grad_part(2 * i + 1)

        slot(count + 1 + i)

    @pl.loop(count + 1 + both, 2 * count)
    def _(s):
        slot(s)

    @pl.loop(jnp.maximum(2 * count - lag, 0), 2 * count)
    def _(s):
        totals(s)

    for t in range(n_tensor):
        send_moments(t).wait_send()
    for t in range(1, n_tensor):
        send_cross(t).wait_send()

    @pl.loop(0, count)
    def _(c):
        pltpu.make_async_copy(n_buf.at[c], normed_out.at[:, columns(c)], n_out.at[c]).wait()
        send_grad(c).wait_send()
        send_grad(c).wait_recv()

    @pl.loop(0, 2 * count)
    def _(s):
        send_up(s).wait_send()

        @pl.when(relay)
        def _():
            send_total(s).wait_send()

        pltpu.make_async_copy(tot.at[s], bias_out.at[:, pl.ds(0, CW)], sum_out.at[s]).wait()


def local(section_out, embedded, cot_norm, cot_res, gain, bias, lang_ids, mb_order):
    n_dp, n_pipe, n_tensor = (lax.axis_size(axis) for axis in ("dp", "pipe", "tensor"))
    tokens, width = embedded.shape
    langs = gain.shape[1]
    per = tokens // MB
    count = width // CW
    dma = pltpu.SemaphoreType.DMA
    normed, grad, gain_grad, bias_grad = pl.pallas_call(
        functools.partial(kernel, n_dp, n_pipe, n_tensor),
        out_shape=(
            jax.ShapeDtypeStruct((tokens, width), BF16),
            jax.ShapeDtypeStruct((tokens, width), BF16),
            jax.ShapeDtypeStruct((langs, width), F32),
            jax.ShapeDtypeStruct((langs, width), F32),
        ),
        in_specs=[ANY, ANY, ANY, ANY, VMEM, VMEM, VMEM, SMEM],
        out_specs=(ANY, ANY, ANY, ANY),
        scratch_shapes=[
            pltpu.VMEM((tokens, width), BF16),
            pltpu.VMEM((MB, per, width), BF16),
            pltpu.VMEM((MB, per, width), BF16),
            pltpu.VMEM((count, tokens, CW), BF16),
            pltpu.VMEM((count, tokens, CW), BF16),
            pltpu.VMEM((count, tokens, CW), F32),
            pltpu.VMEM((count, tokens, CW), F32),
            pltpu.VMEM((count, tokens, CW), BF16),
            pltpu.VMEM((count, tokens, CW), BF16),
            pltpu.VMEM((MB, per, CW), BF16),
            pltpu.VMEM((2 * count, langs, CW), F32),
            pltpu.VMEM((2 * count, langs, CW), F32),
            pltpu.VMEM((2 * count, langs, CW), F32),
            pltpu.VMEM((tokens, LANES), F32),
            pltpu.VMEM((n_tensor, tokens, LANES), F32),
            pltpu.VMEM((tokens, LANES), F32),
            pltpu.VMEM((n_tensor, tokens, LANES), F32),
            pltpu.VMEM((4, tokens, LANES), F32),
            pltpu.VMEM((langs, 2 * tokens), BF16),
            pltpu.VMEM((tokens, langs), BF16),
            dma((3,)), dma((count,)), dma((count,)),
            dma((n_tensor,)), dma((n_tensor,)), dma((n_tensor,)), dma((n_tensor,)),
            dma((2 * count,)), dma((2 * count,)), dma((2 * count,)), dma((2 * count,)),
            dma((2 * count,)), dma((count,)), dma((count,)), dma((count,)),
        ],
        compiler_params=pltpu.CompilerParams(
            collective_id=0, has_side_effects=True, vmem_limit_bytes=56 * 1024 * 1024
        ),
        cost_estimate=pl.CostEstimate(flops=10**9, bytes_accessed=16 * 2**20, transcendentals=0),
    )(
        section_out, embedded,
        cot_norm.reshape(MB, per, width), cot_res.reshape(MB, per, width),
        gain[0], bias[0], lang_ids.reshape(1, tokens), mb_order,
    )
    return normed[None], grad[None], gain_grad[None], bias_grad[None]


def solution(mesh):
    return jax.shard_map(
        local,
        mesh=mesh,
        in_specs=(
            P("pipe", "dp", "tensor"),
            P("dp", "tensor"),
            P("pipe", "dp", "tensor"),
            P("pipe", "dp", "tensor"),
            P("pipe", None, "tensor"),
            P("pipe", None, "tensor"),
            P("dp"),
            P("dp", None),
        ),
        out_specs=(
            P("pipe", "dp", "tensor"),
            P("pipe", "dp", "tensor"),
            P("pipe", None, "tensor"),
            P("pipe", None, "tensor"),
        ),
        check_vma=False,
    )
```

```python
import functools

import jax
import jax.numpy as jnp
from jax import lax
from jax.experimental import pallas as pl
from jax.experimental.pallas import tpu as pltpu
from jax.sharding import PartitionSpec as P

D = 12288
MB = 4
EPS = 1e-05
CW = 384
AHEAD = 4
LANES = 128
MESH = pl.DeviceIdType.MESH
ANY = pl.BlockSpec(memory_space=pl.ANY)
VMEM = pl.BlockSpec(memory_space=pltpu.VMEM)
SMEM = pl.BlockSpec(memory_space=pltpu.SMEM)
F32 = jnp.float32
BF16 = jnp.bfloat16


def fold(value):
    total = value[:, :LANES]
    for start in range(LANES, value.shape[1], LANES):
        total = total + value[:, start : start + LANES]
    return total


def pack(first, second):
    lane = lax.broadcasted_iota(jnp.int32, first.shape, 1)
    one = jnp.sum(first, axis=1, keepdims=True)
    two = jnp.sum(second, axis=1, keepdims=True)
    return jnp.where(lane == 0, one, jnp.where(lane == 1, two, 0.0))


def kernel(
    n_dp, n_pipe, n_tensor,
    section, embedded, cot, res, gain, bias, lang, order,
    normed_out, grad_out, gain_out, bias_out,
    source, cot_raw, res_raw, x_buf, cot_fwd, xn_buf, sc_buf, n_buf, g_buf, g_tmp,
    own, came, tot, mom_own, mom_in, cross_own, cross_in, rows, sel_t2, sel,
    load_sem, x_send, x_recv, mom_send, mom_recv, cross_send, cross_recv,
    up_send, in_recv, tot_send, tot_recv, sum_out, n_out, g_send, g_recv,
):
    dp, pipe, tensor = lax.axis_index("dp"), lax.axis_index("pipe"), lax.axis_index("tensor")
    tokens, width = section.shape[1], section.shape[2]
    langs = gain.shape[0]
    per = tokens // MB
    count = width // CW
    half = n_dp // 2
    lead = min(AHEAD, count)
    left = dp < half
    up = jnp.where(left, dp + 1, dp - 1)
    out = jnp.where(left, dp - 1, dp + 1)
    center = jnp.logical_or(dp == half - 1, dp == half)
    edge = jnp.logical_not(center)
    relay = jnp.logical_and(dp > 0, dp < n_dp - 1)
    after, before = lax.rem(pipe + 1, n_pipe), lax.rem(pipe + n_pipe - 1, n_pipe)
    first, last = pipe == 0, pipe == n_pipe - 1

    def columns(c):
        return pl.ds(pl.multiple_of(c * CW, CW), CW)

    @pl.when(last)
    def _():
        pltpu.make_async_copy(embedded, source, load_sem.at[0]).start()

    @pl.when(jnp.logical_not(last))
    def _():
        pltpu.make_async_copy(section.at[0], source, load_sem.at[0]).start()

    load_cot = pltpu.make_async_copy(cot, cot_raw, load_sem.at[1])
    load_res = pltpu.make_async_copy(res, res_raw, load_sem.at[2])
    load_cot.start()
    load_res.start()

    barrier = pltpu.get_barrier_semaphore()
    partners = 0
    for step in (1, n_dp - 1):
        pl.semaphore_signal(barrier, inc=1, device_id={"dp": lax.rem(dp + step, n_dp)}, device_id_type=MESH)
        partners += 1
    for t in range(n_tensor):
        other = lax.rem(tensor + t, n_tensor)
        for p in (after, before):
            pl.semaphore_signal(barrier, inc=1, device_id={"pipe": p, "tensor": other}, device_id_type=MESH)
            partners += 1
        if t:
            pl.semaphore_signal(barrier, inc=1, device_id={"tensor": other}, device_id_type=MESH)
            partners += 1

    picks = (lax.broadcasted_iota(jnp.int32, (langs, tokens), 0) == lang[...]).astype(F32)
    sel_t2[:, :tokens] = picks.astype(BF16)
    sel_t2[:, tokens:] = picks.astype(BF16)
    sel[...] = picks.T.astype(BF16)

    zeros = jnp.zeros((tokens, LANES), F32)

    def send_moments(t):
        return pltpu.make_async_remote_copy(
            src_ref=mom_own, dst_ref=mom_in.at[tensor],
            send_sem=mom_send.at[t], recv_sem=mom_recv.at[tensor],
            device_id={"pipe": after, "tensor": lax.rem(tensor + t, n_tensor)}, device_id_type=MESH,
        )

    def send_x(c):
        return pltpu.make_async_remote_copy(
            src_ref=section.at[0, :, columns(c)], dst_ref=x_buf.at[c],
            send_sem=x_send.at[c], recv_sem=x_recv.at[c],
            device_id={"pipe": after}, device_id_type=MESH,
        )

    def load_x(c):
        return pltpu.make_async_copy(embedded.at[:, columns(c)], x_buf.at[c], x_recv.at[c])

    def send_up(s):
        return pltpu.make_async_remote_copy(
            src_ref=own.at[s], dst_ref=came.at[s], send_sem=up_send.at[s], recv_sem=in_recv.at[s],
            device_id={"dp": up}, device_id_type=MESH,
        )

    def swap(s):
        return pltpu.make_async_remote_copy(
            src_ref=own.at[s], dst_ref=tot.at[s], send_sem=up_send.at[s], recv_sem=tot_recv.at[s],
            device_id={"dp": up}, device_id_type=MESH,
        )

    def send_total(s):
        return pltpu.make_async_remote_copy(
            src_ref=tot.at[s], dst_ref=tot.at[s], send_sem=tot_send.at[s], recv_sem=tot_recv.at[s],
            device_id={"dp": out}, device_id_type=MESH,
        )

    def partial_on(s):
        @pl.when(relay)
        def _():
            send_up(s).wait_recv()
            own[s] = own[s] + came[s]

        @pl.when(center)
        def _():
            swap(s).start()

        @pl.when(edge)
        def _():
            send_up(s).start()

    def total_on(s, target, c):
        swap(s).wait_recv()

        @pl.when(center)
        def _():
            tot[s] = tot[s] + own[s]

        @pl.when(relay)
        def _():
            send_total(s).start()

        pltpu.make_async_copy(tot.at[s], target.at[:, columns(c)], sum_out.at[s]).start()

    def totals(s):
        @pl.when(s < count)
        def _():
            total_on(s, bias_out, s)

        @pl.when(s >= count)
        def _():
            total_on(s, gain_out, s - count)

    lag = jnp.where(center, 2, 8)
    inner = jnp.logical_or(relay, center)

    def end_sends(s):
        @pl.when(jnp.logical_not(inner))
        def _():
            send_up(s).start()

    def slot(s):
        @pl.when(inner)
        def _():
            partial_on(s)

        @pl.when(jnp.logical_and(jnp.logical_not(inner), s + lead < 2 * count))
        def _():
            send_up(s + lead).start()

        @pl.when(s >= lag)
        def _():
            totals(s - lag)

    slots = [order[0, j] for j in range(MB)]
    place = []
    for m in range(MB):
        found = 0
        for j in range(MB):
            found = jnp.where(slots[j] == m, j, found)
        place.append(found)

    def bias_part(c):
        cols = columns(c)
        for m in range(MB):
            cot_fwd[c, m * per : (m + 1) * per, :] = cot_raw[place[m], :, cols]
        own[c] = jnp.dot(sel_t2[:, :tokens], cot_fwd[c], preferred_element_type=F32)

    def send_first(c):
        end_sends(c)

        @pl.when(jnp.logical_not(last))
        def _():
            send_x(c).start()

    load_cot.wait()
    for c in range(lead):
        bias_part(c)
    pl.semaphore_wait(barrier, partners)
    send_first(0)

    @pl.when(first)
    def _():
        @pl.loop(0, count)
        def _(c):
            load_x(c).start()

    pltpu.make_async_copy(embedded, source, load_sem.at[0]).wait()

    def moments(c, carry):
        x = source[:, columns(c)].astype(F32)
        return carry[0] + fold(x), carry[1] + fold(x * x)

    one, two = lax.fori_loop(0, count, moments, (zeros, zeros))
    mom_own[...] = pack(one, two)
    for t in range(n_tensor):
        send_moments(t).start()
    for c in range(1, lead):
        send_first(c)

    for t in range(n_tensor):
        pltpu.make_async_remote_copy(
            src_ref=mom_own, dst_ref=mom_in.at[t], send_sem=mom_send.at[t], recv_sem=mom_recv.at[t],
            device_id={"pipe": after}, device_id_type=MESH,
        ).wait_recv()
    moment = mom_in[0]
    for t in range(1, n_tensor):
        moment = moment + mom_in[t]
    mean = moment[:, 0:1] / D
    spread = moment[:, 1:2] / D - mean * mean
    rows[0] = jnp.broadcast_to(mean, (tokens, LANES))
    rows[1] = jnp.broadcast_to(lax.rsqrt(spread + EPS), (tokens, LANES))
    cross_in[tensor] = zeros
    rows[2] = zeros
    rows[3] = zeros

    def wide(value):
        return jnp.concatenate([value] * (CW // LANES), axis=1)

    @pl.loop(0, count)
    def _(c):
        cols = columns(c)

        @pl.when(c + lead < count)
        def _():
            bias_part(c + lead)

        slot(c)

        @pl.when(first)
        def _():
            load_x(c).wait()

        @pl.when(jnp.logical_not(first))
        def _():
            send_x(c).wait_recv()

        @pl.when(jnp.logical_not(last))
        def _():
            send_x(c).wait_send()

            @pl.when(c + lead < count)
            def _():
                send_x(c + lead).start()

        gain_rows = jnp.dot(sel[...], gain[:, cols], preferred_element_type=F32)
        bias_rows = jnp.dot(sel[...], bias[:, cols], preferred_element_type=F32)
        xn = (x_buf[c].astype(F32) - wide(rows[0])) * wide(rows[1])
        n_buf[c] = (xn * gain_rows + bias_rows).astype(BF16)
        pltpu.make_async_copy(n_buf.at[c], normed_out.at[:, cols], n_out.at[c]).start()
        ct = cot_fwd[c].astype(F32)
        sc = ct * gain_rows
        rows[2] = rows[2] + fold(sc)
        rows[3] = rows[3] + fold(sc * xn)
        xn_buf[c] = xn
        sc_buf[c] = sc
        product = ct * xn
        high = product.astype(BF16)
        low = (product - high.astype(F32)).astype(BF16)
        own[count + c] = jnp.dot(
            sel_t2[...], jnp.concatenate([high, low], axis=0), preferred_element_type=F32
        )

    cross_own[...] = pack(rows[2], rows[3])

    def send_cross(t):
        return pltpu.make_async_remote_copy(
            src_ref=cross_own, dst_ref=cross_in.at[tensor],
            send_sem=cross_send.at[t], recv_sem=cross_recv.at[tensor],
            device_id={"tensor": lax.rem(tensor + t, n_tensor)}, device_id_type=MESH,
        )

    for t in range(1, n_tensor):
        send_cross(t).start()
    slot(count)
    for t in range(1, n_tensor):
        other = lax.rem(tensor + t, n_tensor)
        pltpu.make_async_remote_copy(
            src_ref=cross_own, dst_ref=cross_in.at[other],
            send_sem=cross_send.at[t], recv_sem=cross_recv.at[other],
            device_id={"tensor": other}, device_id_type=MESH,
        ).wait_recv()
    cross = cross_own[...]
    for t in range(n_tensor):
        cross = cross + cross_in[t]
    rows[2] = jnp.broadcast_to(cross[:, 0:1] / D, (tokens, LANES))
    rows[3] = jnp.broadcast_to(cross[:, 1:2] / D, (tokens, LANES))
    load_res.wait()

    def send_grad(c):
        return pltpu.make_async_remote_copy(
            src_ref=g_buf.at[c], dst_ref=grad_out.at[:, columns(c)],
            send_sem=g_send.at[c], recv_sem=g_recv.at[c],
            device_id={"pipe": before}, device_id_type=MESH,
        )

    def grad_part(c):
        cols = columns(c)
        for m in range(MB):
            span = slice(m * per, (m + 1) * per)
            part = sc_buf[c, span, :] - wide(rows[2, span, :]) - xn_buf[c, span, :] * wide(rows[3, span, :])
            g_tmp[m] = (
                res_raw[place[m], :, cols].astype(F32) + wide(rows[1, span, :]) * part
            ).astype(BF16)
        for j in range(MB):
            g_buf[c, j * per : (j + 1) * per, :] = g_tmp[slots[j]]
        send_grad(c).start()

    both = count // 2

    @pl.loop(0, both)
    def _(i):
        grad_part(2 * i)
        grad_part(2 * i + 1)

        slot(count + 1 + i)

    @pl.loop(count + 1 + both, 2 * count)
    def _(s):
        slot(s)

    @pl.loop(jnp.maximum(2 * count - lag, 0), 2 * count)
    def _(s):
        totals(s)

    for t in range(n_tensor):
        send_moments(t).wait_send()
    for t in range(1, n_tensor):
        send_cross(t).wait_send()

    @pl.loop(0, count)
    def _(c):
        pltpu.make_async_copy(n_buf.at[c], normed_out.at[:, columns(c)], n_out.at[c]).wait()
        send_grad(c).wait_send()
        send_grad(c).wait_recv()

    @pl.loop(0, 2 * count)
    def _(s):
        send_up(s).wait_send()

        @pl.when(relay)
        def _():
            send_total(s).wait_send()

        pltpu.make_async_copy(tot.at[s], bias_out.at[:, pl.ds(0, CW)], sum_out.at[s]).wait()


PIECES = 4


def hand_over(*refs):
    n = (len(refs) - 1) // 2
    sems = refs[-1]
    copies = []
    for k in range(n):
        size = refs[k].shape[0] // PIECES
        for piece in range(PIECES):
            span = pl.ds(piece * size, size)
            copies.append(
                pltpu.make_async_copy(refs[k].at[span], refs[n + k].at[span], sems.at[k * PIECES + piece])
            )
    for copy in copies:
        copy.start()
    for copy in copies:
        copy.wait()


def local(section_out, embedded, cot_norm, cot_res, gain, bias, lang_ids, mb_order):
    n_dp, n_pipe, n_tensor = (lax.axis_size(axis) for axis in ("dp", "pipe", "tensor"))
    tokens, width = embedded.shape
    langs = gain.shape[1]
    per = tokens // MB
    count = width // CW
    dma = pltpu.SemaphoreType.DMA
    normed, grad, gain_grad, bias_grad = pl.pallas_call(
        functools.partial(kernel, n_dp, n_pipe, n_tensor),
        out_shape=(
            jax.ShapeDtypeStruct((tokens, width), BF16),
            jax.ShapeDtypeStruct((tokens, width), BF16),
            jax.ShapeDtypeStruct((langs, width), F32),
            jax.ShapeDtypeStruct((langs, width), F32),
        ),
        in_specs=[ANY, ANY, ANY, ANY, VMEM, VMEM, VMEM, SMEM],
        out_specs=(ANY, ANY, ANY, ANY),
        scratch_shapes=[
            pltpu.VMEM((tokens, width), BF16),
            pltpu.VMEM((MB, per, width), BF16),
            pltpu.VMEM((MB, per, width), BF16),
            pltpu.VMEM((count, tokens, CW), BF16),
            pltpu.VMEM((count, tokens, CW), BF16),
            pltpu.VMEM((count, tokens, CW), F32),
            pltpu.VMEM((count, tokens, CW), F32),
            pltpu.VMEM((count, tokens, CW), BF16),
            pltpu.VMEM((count, tokens, CW), BF16),
            pltpu.VMEM((MB, per, CW), BF16),
            pltpu.VMEM((2 * count, langs, CW), F32),
            pltpu.VMEM((2 * count, langs, CW), F32),
            pltpu.VMEM((2 * count, langs, CW), F32),
            pltpu.VMEM((tokens, LANES), F32),
            pltpu.VMEM((n_tensor, tokens, LANES), F32),
            pltpu.VMEM((tokens, LANES), F32),
            pltpu.VMEM((n_tensor, tokens, LANES), F32),
            pltpu.VMEM((4, tokens, LANES), F32),
            pltpu.VMEM((langs, 2 * tokens), BF16),
            pltpu.VMEM((tokens, langs), BF16),
            dma((3,)), dma((count,)), dma((count,)),
            dma((n_tensor,)), dma((n_tensor,)), dma((n_tensor,)), dma((n_tensor,)),
            dma((2 * count,)), dma((2 * count,)), dma((2 * count,)), dma((2 * count,)),
            dma((2 * count,)), dma((count,)), dma((count,)), dma((count,)),
        ],
        compiler_params=pltpu.CompilerParams(
            collective_id=0, has_side_effects=True, vmem_limit_bytes=36 * 1024 * 1024
        ),
        cost_estimate=pl.CostEstimate(flops=10**9, bytes_accessed=16 * 2**20, transcendentals=0),
    )(
        section_out, embedded,
        cot_norm.reshape(MB, per, width), cot_res.reshape(MB, per, width),
        gain[0], bias[0], lang_ids.reshape(1, tokens), mb_order,
    )
    results = (normed, grad, gain_grad, bias_grad)
    normed, grad, gain_grad, bias_grad = pl.pallas_call(
        hand_over,
        out_shape=tuple(jax.ShapeDtypeStruct(r.shape, r.dtype) for r in results),
        in_specs=[ANY] * 4,
        out_specs=(ANY,) * 4,
        scratch_shapes=[dma((4 * PIECES,))],
        cost_estimate=pl.CostEstimate(flops=0, bytes_accessed=12 * 2**20, transcendentals=0),
    )(*results)
    return normed[None], grad[None], gain_grad[None], bias_grad[None]


def solution(mesh):
    return jax.shard_map(
        local,
        mesh=mesh,
        in_specs=(
            P("pipe", "dp", "tensor"),
            P("dp", "tensor"),
            P("pipe", "dp", "tensor"),
            P("pipe", "dp", "tensor"),
            P("pipe", None, "tensor"),
            P("pipe", None, "tensor"),
            P("dp"),
            P("dp", None),
        ),
        out_specs=(
            P("pipe", "dp", "tensor"),
            P("pipe", "dp", "tensor"),
            P("pipe", None, "tensor"),
            P("pipe", None, "tensor"),
        ),
        check_vma=False,
    )
```

```python
import functools

import jax
import jax.numpy as jnp
from jax import lax
from jax.experimental import pallas as pl
from jax.experimental.pallas import tpu as pltpu
from jax.sharding import PartitionSpec as P

D = 12288
MB = 4
EPS = 1e-05
CW = 384
AHEAD = 4
LANES = 128
MESH = pl.DeviceIdType.MESH
ANY = pl.BlockSpec(memory_space=pl.ANY)
HBM = pl.BlockSpec(memory_space=pltpu.HBM)
F32 = jnp.float32
BF16 = jnp.bfloat16


def fold(value):
    total = value[:, :LANES]
    for start in range(LANES, value.shape[1], LANES):
        total = total + value[:, start : start + LANES]
    return total


def pack(first, second):
    lane = lax.broadcasted_iota(jnp.int32, first.shape, 1)
    one = jnp.sum(first, axis=1, keepdims=True)
    two = jnp.sum(second, axis=1, keepdims=True)
    return jnp.where(lane == 0, one, jnp.where(lane == 1, two, 0.0))


def kernel(
    n_dp, n_pipe, n_tensor,
    section, embedded, cot, res, gain_in, bias_in, lang_in, order_in,
    normed_out, grad_out, gain_out, bias_out,
    source, cot_raw, res_raw, x_buf, cot_fwd, xn_buf, sc_buf, n_buf, g_buf, g_tmp,
    own, came, tot, mom_own, mom_in, cross_own, cross_in, rows, sel_t2, sel, gain, bias, lang, order,
    load_sem, x_send, x_recv, mom_send, mom_recv, cross_send, cross_recv,
    up_send, in_recv, tot_send, tot_recv, sum_out, n_out, g_send, g_recv,
):
    dp, pipe, tensor = lax.axis_index("dp"), lax.axis_index("pipe"), lax.axis_index("tensor")
    tokens, width = section.shape[1], section.shape[2]
    langs = gain.shape[0]
    per = tokens // MB
    count = width // CW
    half = n_dp // 2
    lead = min(AHEAD, count)
    left = dp < half
    up = jnp.where(left, dp + 1, dp - 1)
    out = jnp.where(left, dp - 1, dp + 1)
    center = jnp.logical_or(dp == half - 1, dp == half)
    edge = jnp.logical_not(center)
    relay = jnp.logical_and(dp > 0, dp < n_dp - 1)
    after, before = lax.rem(pipe + 1, n_pipe), lax.rem(pipe + n_pipe - 1, n_pipe)
    first, last = pipe == 0, pipe == n_pipe - 1

    def columns(c):
        return pl.ds(pl.multiple_of(c * CW, CW), CW)

    @pl.when(last)
    def _():
        pltpu.make_async_copy(embedded, source, load_sem.at[0]).start()

    @pl.when(jnp.logical_not(last))
    def _():
        pltpu.make_async_copy(section.at[0], source, load_sem.at[0]).start()

    load_cot = pltpu.make_async_copy(cot, cot_raw, load_sem.at[1])
    load_res = pltpu.make_async_copy(res, res_raw, load_sem.at[2])
    small = (
        pltpu.make_async_copy(lang_in, lang, load_sem.at[3]),
        pltpu.make_async_copy(order_in, order, load_sem.at[4]),
    )
    params = (
        pltpu.make_async_copy(gain_in, gain, load_sem.at[5]),
        pltpu.make_async_copy(bias_in, bias, load_sem.at[6]),
    )
    for copy in small + (load_cot,) + params + (load_res,):
        copy.start()

    barrier = pltpu.get_barrier_semaphore()
    partners = 0
    for step in (1, n_dp - 1):
        pl.semaphore_signal(barrier, inc=1, device_id={"dp": lax.rem(dp + step, n_dp)}, device_id_type=MESH)
        partners += 1
    for t in range(n_tensor):
        other = lax.rem(tensor + t, n_tensor)
        for p in (after, before):
            pl.semaphore_signal(barrier, inc=1, device_id={"pipe": p, "tensor": other}, device_id_type=MESH)
            partners += 1
        if t:
            pl.semaphore_signal(barrier, inc=1, device_id={"tensor": other}, device_id_type=MESH)
            partners += 1

    for copy in small:
        copy.wait()
    picks = (lax.broadcasted_iota(jnp.int32, (langs, tokens), 0) == lang[...]).astype(F32)
    sel_t2[:, :tokens] = picks.astype(BF16)
    sel_t2[:, tokens:] = picks.astype(BF16)
    sel[...] = picks.T.astype(BF16)

    zeros = jnp.zeros((tokens, LANES), F32)

    def send_moments(t):
        return pltpu.make_async_remote_copy(
            src_ref=mom_own, dst_ref=mom_in.at[tensor],
            send_sem=mom_send.at[t], recv_sem=mom_recv.at[tensor],
            device_id={"pipe": after, "tensor": lax.rem(tensor + t, n_tensor)}, device_id_type=MESH,
        )

    def send_x(c):
        return pltpu.make_async_remote_copy(
            src_ref=section.at[0, :, columns(c)], dst_ref=x_buf.at[c],
            send_sem=x_send.at[c], recv_sem=x_recv.at[c],
            device_id={"pipe": after}, device_id_type=MESH,
        )

    def load_x(c):
        return pltpu.make_async_copy(embedded.at[:, columns(c)], x_buf.at[c], x_recv.at[c])

    def send_up(s):
        return pltpu.make_async_remote_copy(
            src_ref=own.at[s], dst_ref=came.at[s], send_sem=up_send.at[s], recv_sem=in_recv.at[s],
            device_id={"dp": up}, device_id_type=MESH,
        )

    def swap(s):
        return pltpu.make_async_remote_copy(
            src_ref=own.at[s], dst_ref=tot.at[s], send_sem=up_send.at[s], recv_sem=tot_recv.at[s],
            device_id={"dp": up}, device_id_type=MESH,
        )

    def send_total(s):
        return pltpu.make_async_remote_copy(
            src_ref=tot.at[s], dst_ref=tot.at[s], send_sem=tot_send.at[s], recv_sem=tot_recv.at[s],
            device_id={"dp": out}, device_id_type=MESH,
        )

    def partial_on(s):
        @pl.when(relay)
        def _():
            send_up(s).wait_recv()
            own[s] = own[s] + came[s]

        @pl.when(center)
        def _():
            swap(s).start()

        @pl.when(edge)
        def _():
            send_up(s).start()

    def total_on(s, target, c):
        swap(s).wait_recv()

        @pl.when(center)
        def _():
            tot[s] = tot[s] + own[s]

        @pl.when(relay)
        def _():
            send_total(s).start()

        pltpu.make_async_copy(tot.at[s], target.at[:, columns(c)], sum_out.at[s]).start()

    def totals(s):
        @pl.when(s < count)
        def _():
            total_on(s, bias_out, s)

        @pl.when(s >= count)
        def _():
            total_on(s, gain_out, s - count)

    lag = jnp.where(center, 2, 8)
    inner = jnp.logical_or(relay, center)

    def end_sends(s):
        @pl.when(jnp.logical_not(inner))
        def _():
            send_up(s).start()

    def slot(s):
        @pl.when(inner)
        def _():
            partial_on(s)

        @pl.when(jnp.logical_and(jnp.logical_not(inner), s + lead < 2 * count))
        def _():
            send_up(s + lead).start()

        @pl.when(s >= lag)
        def _():
            totals(s - lag)

    slots = [order[0, j] for j in range(MB)]
    place = []
    for m in range(MB):
        found = 0
        for j in range(MB):
            found = jnp.where(slots[j] == m, j, found)
        place.append(found)

    def bias_part(c):
        cols = columns(c)
        for m in range(MB):
            cot_fwd[c, m * per : (m + 1) * per, :] = cot_raw[place[m], :, cols]
        own[c] = jnp.dot(sel_t2[:, :tokens], cot_fwd[c], preferred_element_type=F32)

    def send_first(c):
        @pl.when(jnp.logical_not(last))
        def _():
            send_x(c).start()

    load_cot.wait()
    bias_part(0)
    pl.semaphore_wait(barrier, partners)
    send_first(0)
    end_sends(0)
    for c in range(1, lead):
        bias_part(c)
        end_sends(c)

    @pl.when(first)
    def _():
        @pl.loop(0, count)
        def _(c):
            load_x(c).start()

    pltpu.make_async_copy(embedded, source, load_sem.at[0]).wait()

    def moments(c, carry):
        x = source[:, columns(c)].astype(F32)
        return carry[0] + fold(x), carry[1] + fold(x * x)

    one, two = lax.fori_loop(0, count, moments, (zeros, zeros))
    mom_own[...] = pack(one, two)
    for t in range(n_tensor):
        send_moments(t).start()
    for c in range(1, lead):
        send_first(c)

    for t in range(n_tensor):
        pltpu.make_async_remote_copy(
            src_ref=mom_own, dst_ref=mom_in.at[t], send_sem=mom_send.at[t], recv_sem=mom_recv.at[t],
            device_id={"pipe": after}, device_id_type=MESH,
        ).wait_recv()
    moment = mom_in[0]
    for t in range(1, n_tensor):
        moment = moment + mom_in[t]
    mean = moment[:, 0:1] / D
    spread = moment[:, 1:2] / D - mean * mean
    rows[0] = jnp.broadcast_to(mean, (tokens, LANES))
    rows[1] = jnp.broadcast_to(lax.rsqrt(spread + EPS), (tokens, LANES))
    cross_in[tensor] = zeros
    rows[2] = zeros
    rows[3] = zeros
    for copy in params:
        copy.wait()

    def wide(value):
        return jnp.concatenate([value] * (CW // LANES), axis=1)

    @pl.loop(0, count)
    def _(c):
        cols = columns(c)

        @pl.when(c + lead < count)
        def _():
            bias_part(c + lead)

        slot(c)

        @pl.when(first)
        def _():
            load_x(c).wait()

        @pl.when(jnp.logical_not(first))
        def _():
            send_x(c).wait_recv()

        @pl.when(jnp.logical_not(last))
        def _():
            send_x(c).wait_send()

            @pl.when(c + lead < count)
            def _():
                send_x(c + lead).start()

        gain_rows = jnp.dot(sel[...], gain[:, cols], preferred_element_type=F32)
        bias_rows = jnp.dot(sel[...], bias[:, cols], preferred_element_type=F32)
        xn = (x_buf[c].astype(F32) - wide(rows[0])) * wide(rows[1])
        n_buf[c] = (xn * gain_rows + bias_rows).astype(BF16)
        pltpu.make_async_copy(n_buf.at[c], normed_out.at[:, cols], n_out.at[c]).start()
        ct = cot_fwd[c].astype(F32)
        sc = ct * gain_rows
        rows[2] = rows[2] + fold(sc)
        rows[3] = rows[3] + fold(sc * xn)
        xn_buf[c] = xn
        sc_buf[c] = sc
        product = ct * xn
        high = product.astype(BF16)
        low = (product - high.astype(F32)).astype(BF16)
        own[count + c] = jnp.dot(
            sel_t2[...], jnp.concatenate([high, low], axis=0), preferred_element_type=F32
        )

    cross_own[...] = pack(rows[2], rows[3])

    def send_cross(t):
        return pltpu.make_async_remote_copy(
            src_ref=cross_own, dst_ref=cross_in.at[tensor],
            send_sem=cross_send.at[t], recv_sem=cross_recv.at[tensor],
            device_id={"tensor": lax.rem(tensor + t, n_tensor)}, device_id_type=MESH,
        )

    for t in range(1, n_tensor):
        send_cross(t).start()
    for t in range(1, n_tensor):
        other = lax.rem(tensor + t, n_tensor)
        pltpu.make_async_remote_copy(
            src_ref=cross_own, dst_ref=cross_in.at[other],
            send_sem=cross_send.at[t], recv_sem=cross_recv.at[other],
            device_id={"tensor": other}, device_id_type=MESH,
        ).wait_recv()
    cross = cross_own[...]
    for t in range(n_tensor):
        cross = cross + cross_in[t]
    rows[2] = jnp.broadcast_to(cross[:, 0:1] / D, (tokens, LANES))
    rows[3] = jnp.broadcast_to(cross[:, 1:2] / D, (tokens, LANES))
    load_res.wait()

    def send_grad(c):
        return pltpu.make_async_remote_copy(
            src_ref=g_buf.at[c], dst_ref=grad_out.at[:, columns(c)],
            send_sem=g_send.at[c], recv_sem=g_recv.at[c],
            device_id={"pipe": before}, device_id_type=MESH,
        )

    def grad_part(c):
        cols = columns(c)
        for m in range(MB):
            span = slice(m * per, (m + 1) * per)
            part = sc_buf[c, span, :] - wide(rows[2, span, :]) - xn_buf[c, span, :] * wide(rows[3, span, :])
            g_tmp[m] = (
                res_raw[place[m], :, cols].astype(F32) + wide(rows[1, span, :]) * part
            ).astype(BF16)
        for j in range(MB):
            g_buf[c, j * per : (j + 1) * per, :] = g_tmp[slots[j]]
        send_grad(c).start()

    both = count // 2

    @pl.loop(0, both)
    def _(i):
        grad_part(2 * i)
        grad_part(2 * i + 1)

        slot(count + i)

    @pl.loop(count + both, 2 * count)
    def _(s):
        slot(s)

    @pl.loop(jnp.maximum(2 * count - lag, 0), 2 * count)
    def _(s):
        totals(s)

    for t in range(n_tensor):
        send_moments(t).wait_send()
    for t in range(1, n_tensor):
        send_cross(t).wait_send()

    @pl.loop(0, count)
    def _(c):
        pltpu.make_async_copy(n_buf.at[c], normed_out.at[:, columns(c)], n_out.at[c]).wait()
        send_grad(c).wait_send()
        send_grad(c).wait_recv()

    @pl.loop(0, 2 * count)
    def _(s):
        send_up(s).wait_send()

        @pl.when(relay)
        def _():
            send_total(s).wait_send()

        pltpu.make_async_copy(tot.at[s], bias_out.at[:, pl.ds(0, CW)], sum_out.at[s]).wait()


PIECES = 4


def hand_over(*refs):
    n = (len(refs) - 1) // 2
    sems = refs[-1]
    copies = []
    for k in range(n):
        size = refs[k].shape[0] // PIECES
        for piece in range(PIECES):
            span = pl.ds(piece * size, size)
            copies.append(
                pltpu.make_async_copy(refs[k].at[span], refs[n + k].at[span], sems.at[k * PIECES + piece])
            )
    for copy in copies:
        copy.start()
    for copy in copies:
        copy.wait()


def local(section_out, embedded, cot_norm, cot_res, gain, bias, lang_ids, mb_order):
    n_dp, n_pipe, n_tensor = (lax.axis_size(axis) for axis in ("dp", "pipe", "tensor"))
    tokens, width = embedded.shape
    langs = gain.shape[1]
    per = tokens // MB
    count = width // CW
    dma = pltpu.SemaphoreType.DMA
    normed, grad, gain_grad, bias_grad = pl.pallas_call(
        functools.partial(kernel, n_dp, n_pipe, n_tensor),
        out_shape=(
            jax.ShapeDtypeStruct((tokens, width), BF16),
            jax.ShapeDtypeStruct((tokens, width), BF16),
            jax.ShapeDtypeStruct((langs, width), F32),
            jax.ShapeDtypeStruct((langs, width), F32),
        ),
        in_specs=[HBM] * 8,
        out_specs=(ANY, ANY, ANY, ANY),
        scratch_shapes=[
            pltpu.VMEM((tokens, width), BF16),
            pltpu.VMEM((MB, per, width), BF16),
            pltpu.VMEM((MB, per, width), BF16),
            pltpu.VMEM((count, tokens, CW), BF16),
            pltpu.VMEM((count, tokens, CW), BF16),
            pltpu.VMEM((count, tokens, CW), F32),
            pltpu.VMEM((count, tokens, CW), F32),
            pltpu.VMEM((count, tokens, CW), BF16),
            pltpu.VMEM((count, tokens, CW), BF16),
            pltpu.VMEM((MB, per, CW), BF16),
            pltpu.VMEM((2 * count, langs, CW), F32),
            pltpu.VMEM((2 * count, langs, CW), F32),
            pltpu.VMEM((2 * count, langs, CW), F32),
            pltpu.VMEM((tokens, LANES), F32),
            pltpu.VMEM((n_tensor, tokens, LANES), F32),
            pltpu.VMEM((tokens, LANES), F32),
            pltpu.VMEM((n_tensor, tokens, LANES), F32),
            pltpu.VMEM((4, tokens, LANES), F32),
            pltpu.VMEM((langs, 2 * tokens), BF16),
            pltpu.VMEM((tokens, langs), BF16),
            pltpu.VMEM((langs, width), BF16),
            pltpu.VMEM((langs, width), BF16),
            pltpu.VMEM((1, tokens), jnp.int32),
            pltpu.SMEM((1, MB), jnp.int32),
            dma((7,)), dma((count,)), dma((count,)),
            dma((n_tensor,)), dma((n_tensor,)), dma((n_tensor,)), dma((n_tensor,)),
            dma((2 * count,)), dma((2 * count,)), dma((2 * count,)), dma((2 * count,)),
            dma((2 * count,)), dma((count,)), dma((count,)), dma((count,)),
        ],
        compiler_params=pltpu.CompilerParams(
            collective_id=0, has_side_effects=True, vmem_limit_bytes=36 * 1024 * 1024
        ),
        cost_estimate=pl.CostEstimate(flops=10**9, bytes_accessed=16 * 2**20, transcendentals=0),
    )(
        *(
            pltpu.with_memory_space_constraint(array, pltpu.HBM)
            for array in (
                section_out, embedded,
                cot_norm.reshape(MB, per, width), cot_res.reshape(MB, per, width),
                gain[0], bias[0], lang_ids.reshape(1, tokens), mb_order,
            )
        )
    )
    results = (normed, grad, gain_grad, bias_grad)
    normed, grad, gain_grad, bias_grad = pl.pallas_call(
        hand_over,
        out_shape=tuple(jax.ShapeDtypeStruct(r.shape, r.dtype) for r in results),
        in_specs=[ANY] * 4,
        out_specs=(ANY,) * 4,
        scratch_shapes=[dma((4 * PIECES,))],
        compiler_params=pltpu.CompilerParams(vmem_limit_bytes=2 * 1024 * 1024),
        cost_estimate=pl.CostEstimate(flops=0, bytes_accessed=12 * 2**20, transcendentals=0),
    )(*results)
    return normed[None], grad[None], gain_grad[None], bias_grad[None]


def solution(mesh):
    return jax.shard_map(
        local,
        mesh=mesh,
        in_specs=(
            P("pipe", "dp", "tensor"),
            P("dp", "tensor"),
            P("pipe", "dp", "tensor"),
            P("pipe", "dp", "tensor"),
            P("pipe", None, "tensor"),
            P("pipe", None, "tensor"),
            P("dp"),
            P("dp", None),
        ),
        out_specs=(
            P("pipe", "dp", "tensor"),
            P("pipe", "dp", "tensor"),
            P("pipe", None, "tensor"),
            P("pipe", None, "tensor"),
        ),
        check_vma=False,
    )
```

```python
import functools

import jax
import jax.numpy as jnp
from jax import lax
from jax.experimental import pallas as pl
from jax.experimental.pallas import tpu as pltpu
from jax.sharding import PartitionSpec as P

D = 12288
MB = 4
EPS = 1e-05
CW = 384
AHEAD = 4
LANES = 128
MESH = pl.DeviceIdType.MESH
ANY = pl.BlockSpec(memory_space=pl.ANY)
HBM = pl.BlockSpec(memory_space=pltpu.HBM)
F32 = jnp.float32
BF16 = jnp.bfloat16


def fold(value):
    total = value[:, :LANES]
    for start in range(LANES, value.shape[1], LANES):
        total = total + value[:, start : start + LANES]
    return total


def pack(first, second):
    lane = lax.broadcasted_iota(jnp.int32, first.shape, 1)
    one = jnp.sum(first, axis=1, keepdims=True)
    two = jnp.sum(second, axis=1, keepdims=True)
    return jnp.where(lane == 0, one, jnp.where(lane == 1, two, 0.0))


def kernel(
    n_dp, n_pipe, n_tensor,
    section, embedded, cot, res, gain_in, bias_in, lang_in, order_in,
    normed_out, grad_out, gain_out, bias_out,
    source, cot_raw, res_raw, x_buf, cot_fwd, xn_buf, sc_buf, n_buf, g_buf, g_tmp,
    own, came, tot, mom_own, mom_in, cross_own, cross_in, rows, sel_t2, sel, gain, bias, lang, order, picked, split,
    load_sem, x_send, x_recv, mom_send, mom_recv, cross_send, cross_recv,
    up_send, in_recv, tot_send, tot_recv, sum_out, n_out, g_send, g_recv,
):
    dp, pipe, tensor = lax.axis_index("dp"), lax.axis_index("pipe"), lax.axis_index("tensor")
    tokens, width = section.shape[1], section.shape[2]
    langs = gain.shape[0]
    per = tokens // MB
    count = width // CW
    half = n_dp // 2
    lead = min(AHEAD, count)
    left = dp < half
    up = jnp.where(left, dp + 1, dp - 1)
    out = jnp.where(left, dp - 1, dp + 1)
    center = jnp.logical_or(dp == half - 1, dp == half)
    edge = jnp.logical_not(center)
    relay = jnp.logical_and(dp > 0, dp < n_dp - 1)
    after, before = lax.rem(pipe + 1, n_pipe), lax.rem(pipe + n_pipe - 1, n_pipe)
    first, last = pipe == 0, pipe == n_pipe - 1

    def columns(c):
        return pl.ds(pl.multiple_of(c * CW, CW), CW)

    @pl.when(last)
    def _():
        pltpu.make_async_copy(embedded, source, load_sem.at[0]).start()

    @pl.when(jnp.logical_not(last))
    def _():
        pltpu.make_async_copy(section.at[0], source, load_sem.at[0]).start()

    load_cot = pltpu.make_async_copy(cot, cot_raw, load_sem.at[1])
    load_res = pltpu.make_async_copy(res, res_raw, load_sem.at[2])
    small = (
        pltpu.make_async_copy(lang_in, lang, load_sem.at[3]),
        pltpu.make_async_copy(order_in, order, load_sem.at[4]),
    )
    params = (
        pltpu.make_async_copy(gain_in, gain, load_sem.at[5]),
        pltpu.make_async_copy(bias_in, bias, load_sem.at[6]),
    )
    for copy in small + (load_cot,) + params + (load_res,):
        copy.start()

    barrier = pltpu.get_barrier_semaphore()
    partners = 0
    for step in (1, n_dp - 1):
        pl.semaphore_signal(barrier, inc=1, device_id={"dp": lax.rem(dp + step, n_dp)}, device_id_type=MESH)
        partners += 1
    for t in range(n_tensor):
        other = lax.rem(tensor + t, n_tensor)
        for p in (after, before):
            pl.semaphore_signal(barrier, inc=1, device_id={"pipe": p, "tensor": other}, device_id_type=MESH)
            partners += 1
        if t:
            pl.semaphore_signal(barrier, inc=1, device_id={"tensor": other}, device_id_type=MESH)
            partners += 1

    for copy in small:
        copy.wait()
    picks = (lax.broadcasted_iota(jnp.int32, (langs, tokens), 0) == lang[...]).astype(F32)
    sel_t2[:, :tokens] = picks.astype(BF16)
    sel_t2[:, tokens:] = picks.astype(BF16)
    sel[...] = picks.T.astype(BF16)

    zeros = jnp.zeros((tokens, LANES), F32)

    def send_moments(t):
        return pltpu.make_async_remote_copy(
            src_ref=mom_own, dst_ref=mom_in.at[tensor],
            send_sem=mom_send.at[t], recv_sem=mom_recv.at[tensor],
            device_id={"pipe": after, "tensor": lax.rem(tensor + t, n_tensor)}, device_id_type=MESH,
        )

    def send_x(c):
        return pltpu.make_async_remote_copy(
            src_ref=section.at[0, :, columns(c)], dst_ref=x_buf.at[c],
            send_sem=x_send.at[c], recv_sem=x_recv.at[c],
            device_id={"pipe": after}, device_id_type=MESH,
        )

    def load_x(c):
        return pltpu.make_async_copy(embedded.at[:, columns(c)], x_buf.at[c], x_recv.at[c])

    def send_up(s):
        return pltpu.make_async_remote_copy(
            src_ref=own.at[s], dst_ref=came.at[s], send_sem=up_send.at[s], recv_sem=in_recv.at[s],
            device_id={"dp": up}, device_id_type=MESH,
        )

    def swap(s):
        return pltpu.make_async_remote_copy(
            src_ref=own.at[s], dst_ref=tot.at[s], send_sem=up_send.at[s], recv_sem=tot_recv.at[s],
            device_id={"dp": up}, device_id_type=MESH,
        )

    def send_total(s):
        return pltpu.make_async_remote_copy(
            src_ref=tot.at[s], dst_ref=tot.at[s], send_sem=tot_send.at[s], recv_sem=tot_recv.at[s],
            device_id={"dp": out}, device_id_type=MESH,
        )

    def partial_on(s):
        @pl.when(relay)
        def _():
            send_up(s).wait_recv()
            own[s] = own[s] + came[s]

        @pl.when(center)
        def _():
            swap(s).start()

        @pl.when(edge)
        def _():
            send_up(s).start()

    def total_on(s, target, c):
        swap(s).wait_recv()

        @pl.when(center)
        def _():
            tot[s] = tot[s] + own[s]

        @pl.when(relay)
        def _():
            send_total(s).start()

        pltpu.make_async_copy(tot.at[s], target.at[:, columns(c)], sum_out.at[s]).start()

    def totals(s):
        @pl.when(s < count)
        def _():
            total_on(s, bias_out, s)

        @pl.when(s >= count)
        def _():
            total_on(s, gain_out, s - count)

    lag = jnp.where(center, 2, 8)
    inner = jnp.logical_or(relay, center)

    def end_sends(s):
        @pl.when(jnp.logical_not(inner))
        def _():
            send_up(s).start()

    def slot(s):
        @pl.when(inner)
        def _():
            partial_on(s)

        @pl.when(jnp.logical_and(jnp.logical_not(inner), s + lead < 2 * count))
        def _():
            send_up(s + lead).start()

        @pl.when(s >= lag)
        def _():
            totals(s - lag)

    slots = [order[0, j] for j in range(MB)]
    place = []
    for m in range(MB):
        found = 0
        for j in range(MB):
            found = jnp.where(slots[j] == m, j, found)
        place.append(found)

    def bias_part(c):
        cols = columns(c)
        for m in range(MB):
            cot_fwd[c, m * per : (m + 1) * per, :] = cot_raw[place[m], :, cols]
        own[c] = jnp.dot(sel_t2[:, :tokens], cot_fwd[c], preferred_element_type=F32)

    def send_first(c):
        @pl.when(jnp.logical_not(last))
        def _():
            send_x(c).start()

    load_cot.wait()
    bias_part(0)
    pl.semaphore_wait(barrier, partners)
    early = min(2, lead)
    for c in range(early):
        send_first(c)
    end_sends(0)
    for c in range(1, lead):
        bias_part(c)
        end_sends(c)

    @pl.when(first)
    def _():
        @pl.loop(0, count)
        def _(c):
            load_x(c).start()

    pltpu.make_async_copy(embedded, source, load_sem.at[0]).wait()

    def moments(c, carry):
        x = source[:, columns(c)].astype(F32)
        return carry[0] + fold(x), carry[1] + fold(x * x)

    one, two = lax.fori_loop(0, count, moments, (zeros, zeros))
    mom_own[...] = pack(one, two)
    for t in range(n_tensor):
        send_moments(t).start()
    for c in range(early, lead):
        send_first(c)

    for t in range(n_tensor):
        pltpu.make_async_remote_copy(
            src_ref=mom_own, dst_ref=mom_in.at[t], send_sem=mom_send.at[t], recv_sem=mom_recv.at[t],
            device_id={"pipe": after}, device_id_type=MESH,
        ).wait_recv()
    moment = mom_in[0]
    for t in range(1, n_tensor):
        moment = moment + mom_in[t]
    mean = moment[:, 0:1] / D
    spread = moment[:, 1:2] / D - mean * mean
    rows[0] = jnp.broadcast_to(mean, (tokens, LANES))
    rows[1] = jnp.broadcast_to(lax.rsqrt(spread + EPS), (tokens, LANES))
    cross_in[tensor] = zeros
    rows[2] = zeros
    rows[3] = zeros
    for copy in params:
        copy.wait()

    def wide(value):
        return jnp.concatenate([value] * (CW // LANES), axis=1)

    @pl.loop(0, count)
    def _(c):
        cols = columns(c)

        @pl.when(c + lead < count)
        def _():
            bias_part(c + lead)

        slot(c)

        @pl.when(first)
        def _():
            load_x(c).wait()

        @pl.when(jnp.logical_not(first))
        def _():
            send_x(c).wait_recv()

        @pl.when(jnp.logical_not(last))
        def _():
            send_x(c).wait_send()

            @pl.when(c + lead < count)
            def _():
                send_x(c + lead).start()

        picked[0] = jnp.dot(sel[...], gain[:, cols], preferred_element_type=F32)
        picked[1] = jnp.dot(sel[...], bias[:, cols], preferred_element_type=F32)
        for m in range(MB):
            span = slice(m * per, (m + 1) * per)
            gain_rows = picked[0, span, :]
            xn = (x_buf[c, span, :].astype(F32) - wide(rows[0, span, :])) * wide(rows[1, span, :])
            n_buf[c, span, :] = (xn * gain_rows + picked[1, span, :]).astype(BF16)
            ct = cot_fwd[c, span, :].astype(F32)
            sc = ct * gain_rows
            rows[2, span, :] = rows[2, span, :] + fold(sc)
            rows[3, span, :] = rows[3, span, :] + fold(sc * xn)
            xn_buf[c, span, :] = xn
            sc_buf[c, span, :] = sc
            product = ct * xn
            high = product.astype(BF16)
            split[span, :] = high
            split[tokens + m * per : tokens + (m + 1) * per, :] = (product - high.astype(F32)).astype(BF16)
        pltpu.make_async_copy(n_buf.at[c], normed_out.at[:, cols], n_out.at[c]).start()
        own[count + c] = jnp.dot(sel_t2[...], split[...], preferred_element_type=F32)

    cross_own[...] = pack(rows[2], rows[3])

    def send_cross(t):
        return pltpu.make_async_remote_copy(
            src_ref=cross_own, dst_ref=cross_in.at[tensor],
            send_sem=cross_send.at[t], recv_sem=cross_recv.at[tensor],
            device_id={"tensor": lax.rem(tensor + t, n_tensor)}, device_id_type=MESH,
        )

    for t in range(1, n_tensor):
        send_cross(t).start()
    for t in range(1, n_tensor):
        other = lax.rem(tensor + t, n_tensor)
        pltpu.make_async_remote_copy(
            src_ref=cross_own, dst_ref=cross_in.at[other],
            send_sem=cross_send.at[t], recv_sem=cross_recv.at[other],
            device_id={"tensor": other}, device_id_type=MESH,
        ).wait_recv()
    cross = cross_own[...]
    for t in range(n_tensor):
        cross = cross + cross_in[t]
    rows[2] = jnp.broadcast_to(cross[:, 0:1] / D, (tokens, LANES))
    rows[3] = jnp.broadcast_to(cross[:, 1:2] / D, (tokens, LANES))
    load_res.wait()

    def send_grad(c):
        return pltpu.make_async_remote_copy(
            src_ref=g_buf.at[c], dst_ref=grad_out.at[:, columns(c)],
            send_sem=g_send.at[c], recv_sem=g_recv.at[c],
            device_id={"pipe": before}, device_id_type=MESH,
        )

    def grad_part(c):
        cols = columns(c)
        for m in range(MB):
            span = slice(m * per, (m + 1) * per)
            part = sc_buf[c, span, :] - wide(rows[2, span, :]) - xn_buf[c, span, :] * wide(rows[3, span, :])
            g_tmp[m] = (
                res_raw[place[m], :, cols].astype(F32) + wide(rows[1, span, :]) * part
            ).astype(BF16)
        for j in range(MB):
            g_buf[c, j * per : (j + 1) * per, :] = g_tmp[slots[j]]
        send_grad(c).start()

    both = count // 2

    @pl.loop(0, both)
    def _(i):
        grad_part(2 * i)
        grad_part(2 * i + 1)

        slot(count + i)

    @pl.loop(count + both, 2 * count)
    def _(s):
        slot(s)

    @pl.loop(jnp.maximum(2 * count - lag, 0), 2 * count)
    def _(s):
        totals(s)

    for t in range(n_tensor):
        send_moments(t).wait_send()
    for t in range(1, n_tensor):
        send_cross(t).wait_send()

    @pl.loop(0, count)
    def _(c):
        pltpu.make_async_copy(n_buf.at[c], normed_out.at[:, columns(c)], n_out.at[c]).wait()
        send_grad(c).wait_send()
        send_grad(c).wait_recv()

    @pl.loop(0, 2 * count)
    def _(s):
        send_up(s).wait_send()

        @pl.when(relay)
        def _():
            send_total(s).wait_send()

        pltpu.make_async_copy(tot.at[s], bias_out.at[:, pl.ds(0, CW)], sum_out.at[s]).wait()


PIECES = 4


def hand_over(*refs):
    n = (len(refs) - 1) // 2
    sems = refs[-1]
    copies = []
    for k in range(n):
        size = refs[k].shape[0] // PIECES
        for piece in range(PIECES):
            span = pl.ds(piece * size, size)
            copies.append(
                pltpu.make_async_copy(refs[k].at[span], refs[n + k].at[span], sems.at[k * PIECES + piece])
            )
    for copy in copies:
        copy.start()
    for copy in copies:
        copy.wait()


def local(section_out, embedded, cot_norm, cot_res, gain, bias, lang_ids, mb_order):
    n_dp, n_pipe, n_tensor = (lax.axis_size(axis) for axis in ("dp", "pipe", "tensor"))
    tokens, width = embedded.shape
    langs = gain.shape[1]
    per = tokens // MB
    count = width // CW
    dma = pltpu.SemaphoreType.DMA
    normed, grad, gain_grad, bias_grad = pl.pallas_call(
        functools.partial(kernel, n_dp, n_pipe, n_tensor),
        out_shape=(
            jax.ShapeDtypeStruct((tokens, width), BF16),
            jax.ShapeDtypeStruct((tokens, width), BF16),
            jax.ShapeDtypeStruct((langs, width), F32),
            jax.ShapeDtypeStruct((langs, width), F32),
        ),
        in_specs=[HBM] * 8,
        out_specs=(ANY, ANY, ANY, ANY),
        scratch_shapes=[
            pltpu.VMEM((tokens, width), BF16),
            pltpu.VMEM((MB, per, width), BF16),
            pltpu.VMEM((MB, per, width), BF16),
            pltpu.VMEM((count, tokens, CW), BF16),
            pltpu.VMEM((count, tokens, CW), BF16),
            pltpu.VMEM((count, tokens, CW), F32),
            pltpu.VMEM((count, tokens, CW), F32),
            pltpu.VMEM((count, tokens, CW), BF16),
            pltpu.VMEM((count, tokens, CW), BF16),
            pltpu.VMEM((MB, per, CW), BF16),
            pltpu.VMEM((2 * count, langs, CW), F32),
            pltpu.VMEM((2 * count, langs, CW), F32),
            pltpu.VMEM((2 * count, langs, CW), F32),
            pltpu.VMEM((tokens, LANES), F32),
            pltpu.VMEM((n_tensor, tokens, LANES), F32),
            pltpu.VMEM((tokens, LANES), F32),
            pltpu.VMEM((n_tensor, tokens, LANES), F32),
            pltpu.VMEM((4, tokens, LANES), F32),
            pltpu.VMEM((langs, 2 * tokens), BF16),
            pltpu.VMEM((tokens, langs), BF16),
            pltpu.VMEM((langs, width), BF16),
            pltpu.VMEM((langs, width), BF16),
            pltpu.VMEM((1, tokens), jnp.int32),
            pltpu.SMEM((1, MB), jnp.int32),
            pltpu.VMEM((2, tokens, CW), F32),
            pltpu.VMEM((2 * tokens, CW), BF16),
            dma((7,)), dma((count,)), dma((count,)),
            dma((n_tensor,)), dma((n_tensor,)), dma((n_tensor,)), dma((n_tensor,)),
            dma((2 * count,)), dma((2 * count,)), dma((2 * count,)), dma((2 * count,)),
            dma((2 * count,)), dma((count,)), dma((count,)), dma((count,)),
        ],
        compiler_params=pltpu.CompilerParams(
            collective_id=0, has_side_effects=True, vmem_limit_bytes=36 * 1024 * 1024
        ),
        cost_estimate=pl.CostEstimate(flops=10**9, bytes_accessed=16 * 2**20, transcendentals=0),
    )(
        *(
            pltpu.with_memory_space_constraint(array, pltpu.HBM)
            for array in (
                section_out, embedded,
                cot_norm.reshape(MB, per, width), cot_res.reshape(MB, per, width),
                gain[0], bias[0], lang_ids.reshape(1, tokens), mb_order,
            )
        )
    )
    results = (normed, grad, gain_grad, bias_grad)
    normed, grad, gain_grad, bias_grad = pl.pallas_call(
        hand_over,
        out_shape=tuple(jax.ShapeDtypeStruct(r.shape, r.dtype) for r in results),
        in_specs=[ANY] * 4,
        out_specs=(ANY,) * 4,
        scratch_shapes=[dma((4 * PIECES,))],
        compiler_params=pltpu.CompilerParams(vmem_limit_bytes=2 * 1024 * 1024),
        cost_estimate=pl.CostEstimate(flops=0, bytes_accessed=12 * 2**20, transcendentals=0),
    )(*results)
    return normed[None], grad[None], gain_grad[None], bias_grad[None]


def solution(mesh):
    return jax.shard_map(
        local,
        mesh=mesh,
        in_specs=(
            P("pipe", "dp", "tensor"),
            P("dp", "tensor"),
            P("pipe", "dp", "tensor"),
            P("pipe", "dp", "tensor"),
            P("pipe", None, "tensor"),
            P("pipe", None, "tensor"),
            P("dp"),
            P("dp", None),
        ),
        out_specs=(
            P("pipe", "dp", "tensor"),
            P("pipe", "dp", "tensor"),
            P("pipe", None, "tensor"),
            P("pipe", None, "tensor"),
        ),
        check_vma=False,
    )
```
